32 devices in a mesh: row: 8 (over y, x, core), col: 4 (over z).
Axes of the slice: x: 2, y: 2, z: 4, core: 2. Of those that a mesh axis runs over, the one named last changes fastest.
Arguments:
- features: bfloat16 [64, 64, 512], P('row', 'col'), may hold values from -6 to 6
- conv_first: bfloat16 [3, 3, 512, 512], replicated, may hold values from -0.25 to 0.25
- conv_second: bfloat16 [3, 3, 512, 512], replicated, may hold values from -0.09375 to 0.09375
- conv_last: bfloat16 [3, 3, 512, 16], replicated, may hold values from -0.25 to 0.25
- noise: bfloat16 [1024, 64], P(('row', 'col')), may hold values from -6 to 6
- prior_patches: bfloat16 [1024, 3, 64], P(('row', 'col')), may hold values from -6 to 6
- step_index: int32 [4], replicated, may hold values from 0 to 3
- mod_table: float32 [4, 3, 3072], replicated, may hold values from -3 to 3
- embed_weight: bfloat16 [64, 3072], replicated, may hold values from -0.75 to 0.75
- qkv_weight: bfloat16 [3072, 9216], P(None, 'col')
- q_gain: float32 [128], replicated, may hold values from 0.5 to 5
- k_gain: float32 [128], replicated, may hold values from 0.5 to 5
- out_weight: bfloat16 [3072, 3072], P('col'), may hold values from -0.109375 to 0.109375
Outputs:
- block_out: bfloat16 [1024, 4, 3072], P(('row', 'col'))
The draws below stay inside these ranges and needn't reach their ends.
All inputs are finite; a program needn't handle non-finite values.
Results may differ from the reference program's by a relative error of at most 0.017.
Values may be sent and summed in bfloat16 or wider, within the bound.
No kernel may reach another device: no remote copies, remote signals or barrier semaphores. Data moves between devices by JAX's collectives and lax.ppermute only.
A program may use at most 192 MiB of HBM per device.

```python
import math
import jax
import jax.numpy as jnp
from jax import lax

D = 3072
HEADS = 24
HD = 128
ENC = 512
LAT = 16
TH = 8
TW = 16
SLOTS = 4
STEPS = 4
H_IMG = 64
W_IMG = 64
PATCH = 64
TOKENS_SLOT = 1024
N_ROW = 8
N_COL = 4


def draw_qkv_weight(key, part):
    key = jax.random.fold_in(key, 11)
    base = jax.random.normal(key, (D, HEADS, 3, HD), jnp.float32) * D ** (-0.5)
    return base.reshape(D, HEADS * 3 * HD).astype(jnp.bfloat16)


def draw_q_gain(key, part):
    key = jax.random.fold_in(key, 12)
    return jax.random.uniform(key, (HD,), jnp.float32, 0.5, 2.0)


def draw_k_gain(key, part):
    key = jax.random.fold_in(key, 13)
    return jax.random.uniform(key, (HD,), jnp.float32, 0.5, 2.0)


def with_ends(values, key, smallest, largest):
    dims = values.shape
    spot = [jax.random.randint(jax.random.fold_in(key, axis), (), 0, dims[axis]) for axis in range(len(dims))]
    values = values.at[tuple(spot)].set(smallest)
    longest = dims.index(max(dims))
    spot[longest] = (spot[longest] + 1) % dims[longest]
    return values.at[tuple(spot)].set(largest)


def level_of(stream_key, extent, split, least, top_value):
    level, own = 1.0, jax.random.fold_in(stream_key, 6)
    for dim, blocks in split:
        draws = jnp.exp(jax.random.uniform(jax.random.fold_in(own, dim), (blocks,), jnp.float32, least / len(split), top_value / len(split)))
        level = level * jnp.repeat(draws, extent[dim] // blocks).reshape([-1 if axis == dim else 1 for axis in range(len(extent))])
    return level


def scatter_about(stream_key, shape, width, most, cuts=(), dtype=jnp.bfloat16):
    values = width * jax.random.normal(stream_key, shape, jnp.float32)
    if cuts:
        values = values * level_of(stream_key, shape, cuts, -0.22, 0.18)
    return jnp.clip(values, -most, most).astype(dtype)


def setup_inputs(seed: int = 0) -> dict:
    arg_keys = jax.random.split(jax.random.key(seed), 14)
    return {
        "features": scatter_about(arg_keys[0], (H_IMG, W_IMG, ENC), 1.0, 6.0, ((0, 8), (1, 4))),
        "conv_first": scatter_about(arg_keys[1], (3, 3, ENC, ENC), ENC ** -0.5, 0.25),
        "conv_second": scatter_about(arg_keys[2], (3, 3, ENC, ENC), (9 * ENC) ** -0.5, 0.09375),
        "conv_last": scatter_about(arg_keys[3], (3, 3, ENC, LAT), ENC ** -0.5, 0.25),
        "noise": scatter_about(arg_keys[4], (TOKENS_SLOT, PATCH), 1.0, 6.0, ((0, 32),)),
        "prior_patches": scatter_about(arg_keys[5], (TOKENS_SLOT, SLOTS - 1, PATCH), 1.0, 6.0, ((0, 32),)),
        "step_index": with_ends(jax.random.randint(arg_keys[6], (SLOTS,), 0, STEPS), jax.random.fold_in(arg_keys[6], 1), 0, STEPS - 1).astype(jnp.int32),
        "mod_table": scatter_about(arg_keys[7], (STEPS, 3, D), 0.5, 3.0, (), jnp.float32),
        "embed_weight": scatter_about(arg_keys[8], (PATCH, D), PATCH ** -0.5, 0.75),
        "qkv_weight": draw_qkv_weight(jax.random.fold_in(arg_keys[13], 71), 0),
        "q_gain": draw_q_gain(jax.random.fold_in(arg_keys[13], 71), 0),
        "k_gain": draw_k_gain(jax.random.fold_in(arg_keys[13], 71), 0),
        "out_weight": scatter_about(arg_keys[12], (D, D), D ** -0.5, 0.109375, ((0, 4),)),
    }


norm_eps = 1e-06
latent_shift = 0.1159
latent_scale = 0.3611

def conv_same(field, kernel):
    out = lax.conv_general_dilated(lax.optimization_barrier(field).astype(jnp.float32)[None], kernel.astype(jnp.float32), (1, 1), 'SAME', dimension_numbers=('NHWC', 'HWIO', 'NHWC'))
    return out[0]

def swish(field):
    return jax.nn.silu(field.astype(jnp.float32)).astype(jnp.bfloat16)

def rms_scale(values, gain):
    return values * lax.rsqrt(lax.optimization_barrier(jnp.mean(values * values, axis=-1, keepdims=True)) + norm_eps) * gain

def one_head(packed):
    queries, keys, values = packed
    scores = jnp.einsum('sqd,skd->sqk', queries.astype(jnp.float32), keys.astype(jnp.float32)) / math.sqrt(HD)
    top = lax.optimization_barrier(jnp.max(scores, axis=-1, keepdims=True))
    expo = jnp.exp(scores - top)
    weights = lax.optimization_barrier(expo.astype(jnp.bfloat16))
    totals = lax.optimization_barrier(jnp.sum(expo, axis=-1, keepdims=True))
    mixed = jnp.einsum('sqk,skd->sqd', weights.astype(jnp.float32), values.astype(jnp.float32))
    return (mixed / totals).astype(jnp.bfloat16)

def reference(features, conv_first, conv_second, conv_last, noise, prior_patches, step_index, mod_table, embed_weight, qkv_weight, q_gain, k_gain, out_weight):
    act0 = swish(features)
    inner = conv_same(act0, conv_first).astype(jnp.bfloat16)
    act1 = swish(inner)
    block = (features.astype(jnp.float32) + conv_same(act1, conv_second)).astype(jnp.bfloat16)
    act2 = swish(block)
    latent = (conv_same(act2, conv_last) - latent_shift) * latent_scale
    patch = latent.reshape(N_ROW, TH // 2, 2, N_COL, TW // 2, 2, LAT).transpose(0, 3, 1, 4, 2, 5, 6).reshape(TOKENS_SLOT, PATCH)
    sigma = (STEPS - step_index.astype(jnp.float32)) / (STEPS + 1.0)
    fresh = ((1.0 - sigma[0]) * patch + sigma[0] * noise.astype(jnp.float32)).astype(jnp.bfloat16)
    patches = jnp.concatenate([fresh[:, None, :], prior_patches], axis=1)
    mods = mod_table[step_index]
    embedded = jnp.einsum('tsc,cd->tsd', lax.optimization_barrier(patches).astype(jnp.float32), embed_weight.astype(jnp.float32)).astype(jnp.bfloat16)
    embedded = lax.optimization_barrier(embedded)
    hidden = embedded.astype(jnp.float32)
    mean = lax.optimization_barrier(jnp.mean(hidden, axis=-1, keepdims=True))
    centred = hidden - mean
    variance = lax.optimization_barrier(jnp.mean(centred * centred, axis=-1, keepdims=True))
    normed = centred * lax.rsqrt(variance + norm_eps)
    modulated = ((1.0 + mods[None, :, 1, :]) * normed + mods[None, :, 0, :]).astype(jnp.bfloat16)
    modulated = lax.optimization_barrier(modulated)
    qkv = jnp.einsum('tsd,de->tse', modulated.astype(jnp.float32), qkv_weight.astype(jnp.float32))
    qkv = qkv.reshape(TOKENS_SLOT, SLOTS, HEADS, 3, HD)
    queries = rms_scale(qkv[:, :, :, 0], q_gain).astype(jnp.bfloat16)
    keys = rms_scale(qkv[:, :, :, 1], k_gain).astype(jnp.bfloat16)
    values = qkv[:, :, :, 2].astype(jnp.bfloat16)
    packed = (queries.transpose(2, 1, 0, 3), keys.transpose(2, 1, 0, 3), values.transpose(2, 1, 0, 3))
    packed = lax.optimization_barrier(packed)
    attended = lax.map(one_head, packed)
    attended = attended.transpose(2, 1, 0, 3).reshape(TOKENS_SLOT, SLOTS, D)
    attended = lax.optimization_barrier(attended)
    projected = jnp.einsum('tse,ed->tsd', attended.astype(jnp.float32), out_weight.astype(jnp.float32))
    return (embedded.astype(jnp.float32) + mods[None, :, 2, :] * projected).astype(jnp.bfloat16)
```

```python
import functools
import math

import jax
import jax.numpy as jnp
from jax import lax
from jax.experimental import pallas as pl
from jax.experimental.pallas import tpu as pltpu
from jax.sharding import PartitionSpec as P

norm_eps = 1e-06
latent_shift = 0.1159
latent_scale = 0.3611
bf16 = jnp.bfloat16
f32 = jnp.float32


def swish(field):
    return jax.nn.silu(field.astype(f32)).astype(bf16)


def conv_valid(field, kernel):
    out = lax.conv_general_dilated(
        field[None],
        kernel,
        (1, 1),
        "VALID",
        dimension_numbers=("NHWC", "HWIO", "NHWC"),
        preferred_element_type=f32,
    )
    return out[0]


def padded(cells, axis, dim, width):
    count = lax.axis_size(axis)
    head = lax.slice_in_dim(cells, 0, width, axis=dim)
    tail = lax.slice_in_dim(cells, cells.shape[dim] - width, cells.shape[dim], axis=dim)
    before = lax.ppermute(tail, axis, [(i, i + 1) for i in range(count - 1)])
    after = lax.ppermute(head, axis, [(i + 1, i) for i in range(count - 1)])
    return jnp.concatenate([before, cells, after], axis=dim)


def inside(rows, cols, tile_rows, tile_cols, reach):
    at_row = lax.axis_index("row") * tile_rows - reach + jnp.arange(rows)
    at_col = lax.axis_index("col") * tile_cols - reach + jnp.arange(cols)
    ok_row = (at_row >= 0) & (at_row < lax.axis_size("row") * tile_rows)
    ok_col = (at_col >= 0) & (at_col < lax.axis_size("col") * tile_cols)
    return (ok_row[:, None] & ok_col[None, :])[:, :, None]


def encode(wide, conv_first, conv_second, conv_last, tile_rows, tile_cols):
    zero = jnp.zeros((), bf16)
    inner = conv_valid(swish(wide), conv_first).astype(bf16)
    mask = inside(inner.shape[0], inner.shape[1], tile_rows, tile_cols, 2)
    act1 = jnp.where(mask, swish(inner), zero)
    block = (wide[2:-2, 2:-2].astype(f32) + conv_valid(act1, conv_second)).astype(bf16)
    mask = inside(block.shape[0], block.shape[1], tile_rows, tile_cols, 1)
    act2 = jnp.where(mask, swish(block), zero)
    return (conv_valid(act2, conv_last) - latent_shift) * latent_scale


def fold_kernel(e_ref, scale_ref, shift_ref, w_ref, out_ref, lhs_ref):
    slots = scale_ref.shape[0]
    width = e_ref.shape[0]

    @pl.when(pl.program_id(0) == 0)
    def _():
        e = e_ref[...].astype(f32)
        e = e - jnp.mean(e, axis=1, keepdims=True)
        for s in range(slots):
            lhs_ref[s * width : (s + 1) * width, :] = (e * (1.0 + scale_ref[s : s + 1, :])).astype(
                bf16
            )
        lhs_ref[slots * width :, :] = shift_ref[...]

    r = jnp.dot(lhs_ref[...], w_ref[...], preferred_element_type=f32)
    base = slots * width
    for s in range(slots):
        out_ref[0, s, 0:width, :] = r[s * width : (s + 1) * width]
        bias = r[base + s : base + s + 1] + r[base + slots + s : base + slots + s + 1]
        out_ref[0, s, width:, :] = jnp.broadcast_to(bias, (8, bias.shape[1]))


def fold(embed_weight, scale, shift, qkv_weight, head_dim):
    width, depth = embed_weight.shape
    slots = scale.shape[0]
    cols = 3 * head_dim
    heads = qkv_weight.shape[1] // cols
    rows = slots * width + shift.shape[0]
    return pl.pallas_call(
        fold_kernel,
        grid=(heads,),
        in_specs=[
            pl.BlockSpec((width, depth), lambda h: (0, 0)),
            pl.BlockSpec((slots, depth), lambda h: (0, 0)),
            pl.BlockSpec(shift.shape, lambda h: (0, 0)),
            pl.BlockSpec((depth, cols), lambda h: (0, h)),
        ],
        out_specs=pl.BlockSpec((1, slots, width + 8, cols), lambda h: (h, 0, 0, 0)),
        out_shape=jax.ShapeDtypeStruct((heads, slots, width + 8, cols), f32),
        scratch_shapes=[pltpu.VMEM((rows, depth), bf16)],
        compiler_params=pltpu.CompilerParams(vmem_limit_bytes=24 * 2**20),
        cost_estimate=pl.CostEstimate(
            flops=2 * rows * depth * heads * cols,
            bytes_accessed=depth * heads * cols * 2,
            transcendentals=0,
        ),
    )(embed_weight, scale, shift, qkv_weight)


def widen(p, gram_ref):
    pf = p.astype(f32)
    pg = jnp.dot(p, gram_ref[0], preferred_element_type=f32)
    pg = pg + jnp.dot(p, gram_ref[1], preferred_element_type=f32)
    var = jnp.sum(pg * pf, axis=1, keepdims=True)
    pn = pf * lax.rsqrt(jnp.maximum(var, 0.0) + norm_eps)
    hi = pn.astype(bf16)
    lo = (pn - hi.astype(f32)).astype(bf16)
    lane = lax.broadcasted_iota(jnp.int32, p.shape, 1)
    ones = jnp.where(lane < 2, 1.0, 0.0).astype(bf16)
    return jnp.concatenate([hi, lo, hi, ones], axis=1)


def attend_kernel(
    hp, head_dim, key_ref, query_ref, gram_ref, m_ref, gain_ref, wo_ref, keep_ref, send_ref,
    kaug_ref, qaug_ref, acc_ref,
):
    step = pl.program_id(0)
    width = key_ref.shape[-1]

    @pl.when(step == 0)
    def _():
        kaug_ref[...] = widen(key_ref[...].reshape(-1, width), gram_ref)
        qaug_ref[...] = widen(query_ref[...].reshape(-1, width), gram_ref)

    kaug = kaug_ref[...]
    qaug = qaug_ref[...]
    outs = []
    for j in range(hp):
        m = m_ref[j, 0:width, :]
        bias = m_ref[j, width : width + 1, :]
        mhi = m.astype(bf16)
        mlo = (m - mhi.astype(f32)).astype(bf16)
        bhi = bias.astype(bf16).astype(f32)
        blo = bias - bhi
        at = lax.broadcasted_iota(jnp.int32, m.shape, 0)
        low = jnp.where(at == 0, bhi, jnp.where(at == 1, blo, 0.0)).astype(bf16)
        maug = jnp.concatenate([mhi, mhi, mlo, low], axis=0)
        xq = jnp.dot(qaug, maug[:, :head_dim], preferred_element_type=f32)
        xkv = jnp.dot(kaug, maug[:, head_dim:], preferred_element_type=f32)
        xk = xkv[:, :head_dim]
        v = xkv[:, head_dim:].astype(bf16)
        k = (
            xk * lax.rsqrt(jnp.mean(xk * xk, axis=1, keepdims=True) + norm_eps)
        ).astype(bf16)
        q = (
            xq * lax.rsqrt(jnp.mean(xq * xq, axis=1, keepdims=True) + norm_eps) * gain_ref[...]
        ).astype(bf16)
        s = lax.dot_general(q, k, (((1,), (1,)), ((), ())), preferred_element_type=f32)
        e = jnp.exp2(s - jnp.max(s, axis=1, keepdims=True))
        total = jnp.sum(e, axis=1, keepdims=True)
        o = jnp.dot(e.astype(bf16), v, preferred_element_type=f32)
        outs.append((o / total).astype(bf16))
    att = outs[0] if hp == 1 else jnp.concatenate(outs, axis=1)
    part = jnp.dot(att, wo_ref[...], preferred_element_type=f32)

    @pl.when(step == 0)
    def _():
        acc_ref[...] = part

    @pl.when(step > 0)
    def _():
        acc_ref[...] += part

    @pl.when(step == pl.num_programs(0) - 1)
    def _():
        tok = keep_ref.shape[1]
        for i in range(keep_ref.shape[0]):
            keep_ref[i] = acc_ref[2 * i * tok : (2 * i + 1) * tok, :]
            send_ref[i] = acc_ref[(2 * i + 1) * tok : (2 * i + 2) * tok, :].astype(bf16)


def attend(keys, queries, at, gram, folded, slot, gain, out_weight):
    nr, nc, _, tok, width = keys.shape
    heads, _, mrows, cols = folded.shape
    head_dim = cols // 3
    depth = out_weight.shape[1]
    hp = 2 if heads % 2 == 0 else 1
    nk, nq = nr * nc * tok, nc * tok
    half = nc // 2
    return pl.pallas_call(
        functools.partial(attend_kernel, hp, head_dim),
        grid=(heads // hp,),
        in_specs=[
            pl.BlockSpec((nr, nc, None, tok, width), lambda h: (0, 0, at, 0, 0)),
            pl.BlockSpec((nc, None, tok, width), lambda h: (0, at, 0, 0)),
            pl.BlockSpec((2, width, width), lambda h: (0, 0, 0)),
            pl.BlockSpec((hp, None, mrows, cols), lambda h: (h, slot, 0, 0)),
            pl.BlockSpec((1, head_dim), lambda h: (0, 0)),
            pl.BlockSpec((hp * head_dim, depth), lambda h: (h, 0)),
        ],
        out_specs=[
            pl.BlockSpec((half, tok, depth), lambda h: (0, 0, 0)),
            pl.BlockSpec((half, tok, depth), lambda h: (0, 0, 0)),
        ],
        out_shape=[
            jax.ShapeDtypeStruct((half, tok, depth), f32),
            jax.ShapeDtypeStruct((half, tok, depth), bf16),
        ],
        scratch_shapes=[
            pltpu.VMEM((nk, 4 * width), bf16),
            pltpu.VMEM((nq, 4 * width), bf16),
            pltpu.VMEM((nq, depth), f32),
        ],
        compiler_params=pltpu.CompilerParams(vmem_limit_bytes=40 * 2**20),
        cost_estimate=pl.CostEstimate(
            flops=2 * heads * (nk * 256 * 256 + 2 * nq * nk * head_dim * 2 + nq * head_dim * depth),
            bytes_accessed=heads * head_dim * depth * 2 + nq * depth * 3,
            transcendentals=heads * nq * nk,
        ),
    )(keys, queries, gram, folded, gain, out_weight)


def exchange(value, axis, bit):
    count = lax.axis_size(axis)
    return lax.ppermute(value, axis, [(i, i ^ bit) for i in range(count)])


def gather_tokens(own):
    nc = lax.axis_size("col")
    queries = jnp.stack([own] + [exchange(own, "col", k) for k in range(1, nc)])
    return queries, lax.all_gather(queries, "row", axis=0, tiled=False)


def settle(keep, send):
    bit = 1
    while True:
        total = keep + exchange(send, "col", bit).astype(f32)
        if total.shape[0] == 1:
            return total[0]
        keep, send = total[0::2], total[1::2].astype(bf16)
        bit *= 2


def on_device(
    features,
    conv_first,
    conv_second,
    conv_last,
    noise,
    prior_patches,
    step_index,
    mod_table,
    embed_weight,
    qkv_weight,
    q_gain,
    k_gain,
    out_weight,
):
    tile_rows, tile_cols, _ = features.shape
    wide = padded(padded(features, "row", 0, 3), "col", 1, 3)
    prior = prior_patches.transpose(1, 0, 2)
    prior_queries, prior_keys = gather_tokens(prior)

    step_total = mod_table.shape[0]
    mods = sum(
        jnp.where((step_index == k)[:, None, None], mod_table[k][None], 0.0)
        for k in range(step_total)
    )
    slots = step_index.shape[0]
    shift = mods[:, 0, :]
    shift_hi = shift.astype(bf16)
    shift_lo = (shift - shift_hi.astype(f32)).astype(bf16)
    spare = -(2 * slots) % 16
    shift2 = jnp.concatenate(
        [shift_hi, shift_lo, jnp.zeros((spare, shift.shape[1]), bf16)], axis=0
    )
    head_dim = q_gain.shape[0]
    folded = fold(embed_weight, mods[:, 1, :], shift2, qkv_weight, head_dim)
    centred = embed_weight.astype(f32)
    centred = centred - jnp.mean(centred, axis=1, keepdims=True)
    gram = (
        jnp.einsum("ad,bd->ab", centred, centred, precision=lax.Precision.HIGHEST)
        / embed_weight.shape[1]
    )
    gram_hi = gram.astype(bf16)
    gram2 = jnp.stack([gram_hi, (gram - gram_hi.astype(f32)).astype(bf16)])
    gain = (q_gain * k_gain * (math.log2(math.e) / math.sqrt(head_dim)))[None]

    sums = {}
    for slot in range(1, slots):
        keep, send = attend(
            prior_keys, prior_queries, slot - 1, gram2, folded, slot, gain, out_weight
        )
        sums[slot] = settle(keep, send)

    latent = encode(wide, conv_first, conv_second, conv_last, tile_rows, tile_cols)
    channels = latent.shape[-1]
    tok = tile_rows // 2 * (tile_cols // 2)
    patch = (
        latent.reshape(tile_rows // 2, 2, tile_cols // 2, 2, channels)
        .transpose(0, 2, 1, 3, 4)
        .reshape(tok, 4 * channels)
    )
    sigma = (step_total - step_index.astype(f32)) / (step_total + 1.0)
    fresh = ((1.0 - sigma[0]) * patch + sigma[0] * noise.astype(f32)).astype(bf16)
    fresh_queries, fresh_keys = gather_tokens(fresh[None])
    keep, send = attend(fresh_keys, fresh_queries, 0, gram2, folded, 0, gain, out_weight)
    sums[0] = settle(keep, send)

    patches = jnp.concatenate([fresh[None], prior], axis=0)
    own = jnp.einsum(
        "stc,cd->std", patches, embed_weight, preferred_element_type=f32
    ).astype(bf16)
    outs = [
        (own[s].astype(f32) + mods[s, 2][None, :] * sums[s]).astype(bf16) for s in range(slots)
    ]
    return jnp.stack(outs, axis=1)


def solution(mesh):
    placed = (
        P("row", "col", None),
        P(),
        P(),
        P(),
        P(("row", "col"), None),
        P(("row", "col"), None, None),
        P(),
        P(),
        P(),
        P(None, "col"),
        P(),
        P(),
        P("col", None),
    )
    return jax.shard_map(
        on_device,
        mesh=mesh,
        in_specs=placed,
        out_specs=P(("row", "col"), None, None),
        check_vma=False,
    )
```

```python
import functools
import math

import jax
import jax.numpy as jnp
from jax import lax
from jax.experimental import pallas as pl
from jax.experimental.pallas import tpu as pltpu
from jax.sharding import PartitionSpec as P

norm_eps = 1e-06
latent_shift = 0.1159
latent_scale = 0.3611
bf16 = jnp.bfloat16
f32 = jnp.float32


def swish(field):
    return (field / (1.0 + jnp.exp(-field))).astype(bf16)


def shifted(dst_ref, act):
    cols, rows, _ = act.shape
    dst_ref[0, 0:cols] = pltpu.roll(act, 1, 1).astype(bf16)
    dst_ref[1, 0:cols] = act.astype(bf16)
    dst_ref[2, 0:cols] = pltpu.roll(act, rows - 1, 1).astype(bf16)


def encode_kernel(
    place_ref, left_ref, mid_ref, right_ref, f0_ref, f1_ref, f2_ref, s0_ref, s1_ref, s2_ref,
    last_ref, out_ref, x_ref, s_ref, acc_ref,
):
    step = pl.program_id(0)
    wide, rows, channels = x_ref.shape
    tile_cols, tile_rows, _ = out_ref.shape
    first_ref = (f0_ref, f1_ref, f2_ref)
    second_ref = (s0_ref, s1_ref, s2_ref)

    def masked(act, reach):
        shape = act.shape
        col = lax.broadcasted_iota(jnp.int32, shape, 0) + (place_ref[1] - reach)
        row = lax.broadcasted_iota(jnp.int32, shape, 1)
        row = jnp.where(row < tile_rows + 3, row, row - rows) + place_ref[0]
        ok = (row >= 0) & (row < place_ref[2]) & (col >= 0) & (col < place_ref[3])
        return jnp.where(ok, act, 0.0)

    def taps(w_ref, dy, cols):
        total = None
        for dx in range(3):
            lhs = s_ref[dy, dx : dx + cols].reshape(cols * rows, channels)
            part = jnp.dot(lhs, w_ref[dx][...], preferred_element_type=f32)
            total = part if total is None else total + part
        return total.reshape(cols, rows, total.shape[-1])

    @pl.when(step == 0)
    def _():
        x_ref[0:3] = left_ref[...].astype(f32)
        x_ref[3 : 3 + tile_cols] = mid_ref[...].astype(f32)
        x_ref[3 + tile_cols :] = right_ref[...].astype(f32)
        shifted(s_ref, swish(x_ref[...]).astype(f32))
        acc_ref[...] = taps(first_ref, 0, wide - 2)

    for dy in (1, 2):

        @pl.when(step == dy)
        def _():
            acc_ref[...] += taps(first_ref, dy, wide - 2)

    @pl.when(step == 2)
    def _():
        inner = acc_ref[...].astype(bf16).astype(f32)
        shifted(s_ref, masked(swish(inner).astype(f32), 2))

    @pl.when(step == 3)
    def _():
        acc_ref[0 : wide - 4] = x_ref[2 : wide - 2] + taps(second_ref, 0, wide - 4)

    for dy in (1, 2):

        @pl.when(step == 3 + dy)
        def _():
            acc_ref[0 : wide - 4] += taps(second_ref, dy, wide - 4)

    @pl.when(step == 5)
    def _():
        block = acc_ref[0 : wide - 4].astype(bf16).astype(f32)
        shifted(s_ref, masked(swish(block).astype(f32), 1))
        latent = None
        for dy in range(3):
            for dx in range(3):
                lhs = s_ref[dy, dx : dx + wide - 6].reshape(-1, channels)
                part = lax.dot_general(
                    lhs, last_ref[dy, dx], (((1,), (1,)), ((), ())), preferred_element_type=f32
                )
                latent = part if latent is None else latent + part
        latent = ((latent - latent_shift) * latent_scale).reshape(tile_cols, rows, -1)
        out_ref[...] = latent[:, :tile_rows]


def edges(features):
    nr = lax.axis_size("row")
    turned = features.transpose(1, 0, 2)
    tile_cols, tile_rows, channels = turned.shape
    above = lax.ppermute(turned[:, -3:], "row", [(i, i + 1) for i in range(nr - 1)])
    below = lax.ppermute(turned[:, :3], "row", [(i + 1, i) for i in range(nr - 1)])
    spare = -(tile_rows + 6) % 16
    gap = jnp.zeros((tile_cols, spare, channels), bf16)
    return jnp.concatenate([turned, below, gap, above], axis=1)


def sides(mid):
    nc = lax.axis_size("col")
    left = lax.ppermute(mid[-3:], "col", [(i, i + 1) for i in range(nc - 1)])
    right = lax.ppermute(mid[:3], "col", [(i + 1, i) for i in range(nc - 1)])
    return left, right


def encode(left, mid, right, tile_rows, conv_first, conv_second, conv_last):
    nr, nc = lax.axis_size("row"), lax.axis_size("col")
    tile_cols, rows, channels = mid.shape
    wide = tile_cols + 6
    place = jnp.stack(
        [
            lax.axis_index("row") * tile_rows,
            lax.axis_index("col") * tile_cols,
            nr * tile_rows,
            nc * tile_cols,
        ]
    ).astype(jnp.int32)
    hidden = conv_first.shape[3]
    latents = conv_last.shape[3]
    last = conv_last.transpose(0, 1, 3, 2)

    def whole(array):
        return pl.BlockSpec(array.shape, lambda i: (0,) * array.ndim)

    return pl.pallas_call(
        encode_kernel,
        grid=(6,),
        in_specs=[
            pl.BlockSpec(memory_space=pltpu.SMEM),
            whole(left),
            whole(mid),
            whole(right),
            *[
                pl.BlockSpec(
                    (None, None, channels, hidden), lambda i, x=x: (jnp.minimum(i, 2), x, 0, 0)
                )
                for x in range(3)
            ],
            *[
                pl.BlockSpec(
                    (None, None, hidden, channels), lambda i, x=x: (jnp.clip(i - 3, 0, 2), x, 0, 0)
                )
                for x in range(3)
            ],
            whole(last),
        ],
        out_specs=pl.BlockSpec((tile_cols, tile_rows, latents), lambda i: (0, 0, 0)),
        out_shape=jax.ShapeDtypeStruct((tile_cols, tile_rows, latents), f32),
        scratch_shapes=[
            pltpu.VMEM((wide, rows, channels), f32),
            pltpu.VMEM((3, wide, rows, channels), bf16),
            pltpu.VMEM((wide - 2, rows, channels), f32),
        ],
        compiler_params=pltpu.CompilerParams(vmem_limit_bytes=40 * 2**20),
        cost_estimate=pl.CostEstimate(
            flops=2 * 9 * wide * rows * channels * (2 * hidden + latents),
            bytes_accessed=9 * channels * 2 * (2 * hidden + 128),
            transcendentals=3 * wide * rows * channels,
        ),
    )(place, left, mid, right, *[conv_first] * 3, *[conv_second] * 3, last)


def widen(p, gram_ref):
    pf = p.astype(f32)
    pg = jnp.dot(p, gram_ref[0], preferred_element_type=f32)
    pg = pg + jnp.dot(p, gram_ref[1], preferred_element_type=f32)
    var = jnp.sum(pg * pf, axis=1, keepdims=True)
    pn = pf * lax.rsqrt(jnp.maximum(var, 0.0) + norm_eps)
    hi = pn.astype(bf16)
    lo = (pn - hi.astype(f32)).astype(bf16)
    lane = lax.broadcasted_iota(jnp.int32, p.shape, 1)
    ones = jnp.where(lane < 2, 1.0, 0.0).astype(bf16)
    return jnp.concatenate([hi, lo, hi, ones], axis=1)


def attend_kernel(
    hp, head_dim, slot, slots, key_ref, query_ref, gram_ref, m_ref, bias_ref, gain_ref,
    wo_ref, keep_ref, send_ref, kaug_ref, qaug_ref, acc_ref,
):
    step = pl.program_id(0)
    width = key_ref.shape[-1]

    @pl.when(step == 0)
    def _():
        kaug_ref[...] = widen(key_ref[...].reshape(-1, width), gram_ref)
        qaug_ref[...] = widen(query_ref[...].reshape(-1, width), gram_ref)

    kaug = kaug_ref[...]
    qaug = qaug_ref[...]
    outs = []
    for j in range(hp):
        cols = slice(j * 3 * head_dim, (j + 1) * 3 * head_dim)
        m = m_ref[:, cols]
        bias = bias_ref[slot : slot + 1, cols] + bias_ref[slots + slot : slots + slot + 1, cols]
        mhi = m.astype(bf16)
        mlo = (m - mhi.astype(f32)).astype(bf16)
        bhi = bias.astype(bf16).astype(f32)
        blo = bias - bhi
        at = lax.broadcasted_iota(jnp.int32, m.shape, 0)
        low = jnp.where(at == 0, bhi, jnp.where(at == 1, blo, 0.0)).astype(bf16)
        maug = jnp.concatenate([mhi, mhi, mlo, low], axis=0)
        xq = jnp.dot(qaug, maug[:, :head_dim], preferred_element_type=f32)
        xkv = jnp.dot(kaug, maug[:, head_dim:], preferred_element_type=f32)
        xk = xkv[:, :head_dim]
        v = xkv[:, head_dim:].astype(bf16)
        k = (
            xk * lax.rsqrt(jnp.mean(xk * xk, axis=1, keepdims=True) + norm_eps)
        ).astype(bf16)
        q = (
            xq * lax.rsqrt(jnp.mean(xq * xq, axis=1, keepdims=True) + norm_eps) * gain_ref[...]
        ).astype(bf16)
        s = lax.dot_general(q, k, (((1,), (1,)), ((), ())), preferred_element_type=f32)
        e = jnp.exp2(s - jnp.max(s, axis=1, keepdims=True))
        total = jnp.sum(e, axis=1, keepdims=True)
        o = jnp.dot(e.astype(bf16), v, preferred_element_type=f32)
        outs.append((o / total).astype(bf16))
    att = outs[0] if hp == 1 else jnp.concatenate(outs, axis=1)
    part = jnp.dot(att, wo_ref[...], preferred_element_type=f32)

    @pl.when(step == 0)
    def _():
        acc_ref[...] = part

    @pl.when(step > 0)
    def _():
        acc_ref[...] += part

    @pl.when(step == pl.num_programs(0) - 1)
    def _():
        tok = keep_ref.shape[1]
        for i in range(keep_ref.shape[0]):
            keep_ref[i] = acc_ref[2 * i * tok : (2 * i + 1) * tok, :]
            send_ref[i] = acc_ref[(2 * i + 1) * tok : (2 * i + 2) * tok, :].astype(bf16)


def attend(keys, queries, slot, at, gram, folded, gain, out_weight):
    nr, nc, _, tok, width = keys.shape
    slots = folded.shape[0] // width
    head_dim = gain.shape[1]
    heads = folded.shape[1] // (3 * head_dim)
    depth = out_weight.shape[1]
    hp = heads_per_step(heads)
    nk, nq = nr * nc * tok, nc * tok
    half = nc // 2
    spare = folded.shape[0] - slots * width
    out_spec = pl.BlockSpec((half, tok, depth), lambda h: (0, 0, 0))
    return pl.pallas_call(
        functools.partial(attend_kernel, hp, head_dim, slot, slots),
        grid=(heads // hp,),
        in_specs=[
            pl.BlockSpec((nr, nc, None, tok, width), lambda h: (0, 0, at, 0, 0)),
            pl.BlockSpec((nc, None, tok, width), lambda h: (0, at, 0, 0)),
            pl.BlockSpec((2, width, width), lambda h: (0, 0, 0)),
            pl.BlockSpec((width, hp * 3 * head_dim), lambda h: (slot, h)),
            pl.BlockSpec((spare, hp * 3 * head_dim), lambda h: (slots * width // spare, h)),
            pl.BlockSpec((1, head_dim), lambda h: (0, 0)),
            pl.BlockSpec((hp * head_dim, depth), lambda h: (h, 0)),
        ],
        out_specs=[out_spec, out_spec],
        out_shape=[
            jax.ShapeDtypeStruct((half, tok, depth), f32),
            jax.ShapeDtypeStruct((half, tok, depth), bf16),
        ],
        scratch_shapes=[
            pltpu.VMEM((nk, 4 * width), bf16),
            pltpu.VMEM((nq, 4 * width), bf16),
            pltpu.VMEM((nq, depth), f32),
        ],
        compiler_params=pltpu.CompilerParams(vmem_limit_bytes=40 * 2**20),
        cost_estimate=pl.CostEstimate(
            flops=2 * heads * (nk * 256 * 256 + 2 * nq * nk * head_dim * 2 + nq * head_dim * depth),
            bytes_accessed=heads * head_dim * depth * 2 + nq * depth * 3,
            transcendentals=heads * nq * nk,
        ),
    )(keys, queries, gram, folded, folded, gain, out_weight)


def heads_per_step(heads):
    return max(k for k in (1, 2, 3) if heads % k == 0)


def exchange(value, axis, bit):
    count = lax.axis_size(axis)
    return lax.ppermute(value, axis, [(i, i ^ bit) for i in range(count)])


def spread(value, axis, bits):
    masks = [0]
    for bit in bits:
        masks += [mask | bit for mask in masks]
    return jnp.stack([value] + [exchange(value, axis, mask) for mask in masks[1:]])


def bits_of(axis):
    return [1 << i for i in range(lax.axis_size(axis).bit_length() - 1)]


def finish_row(keys, shape):
    rest = bits_of("row")[1:]
    while rest:
        keys = spread(keys, "row", rest[:2]).reshape(-1, *shape)
        rest = rest[2:]
    return keys


def fold_inputs(embed_weight, scale, shift):
    centred = embed_weight.astype(f32)
    centred = centred - jnp.mean(centred, axis=1, keepdims=True)
    width, depth = embed_weight.shape
    slots = scale.shape[0]
    scaled = ((1.0 + scale)[:, None, :] * centred[None]).astype(bf16).reshape(slots * width, depth)
    shift_hi = shift.astype(bf16)
    shift_lo = (shift - shift_hi.astype(f32)).astype(bf16)
    spare = -(2 * slots) % 16
    lhs = jnp.concatenate([scaled, shift_hi, shift_lo, jnp.zeros((spare, depth), bf16)], axis=0)
    gram = jnp.einsum("ad,bd->ab", centred, centred, precision=lax.Precision.HIGHEST) / depth
    gram_hi = gram.astype(bf16)
    return lhs, jnp.stack([gram_hi, (gram - gram_hi.astype(f32)).astype(bf16)])


def on_device(
    features,
    conv_first,
    conv_second,
    conv_last,
    noise,
    prior_patches,
    step_index,
    mod_table,
    embed_weight,
    qkv_weight,
    q_gain,
    k_gain,
    out_weight,
):
    tie = lax.optimization_barrier
    tile_rows, tile_cols, _ = features.shape
    slots = step_index.shape[0]
    prior = prior_patches.transpose(1, 0, 2)
    queries = spread(prior, "col", bits_of("col"))
    mid = edges(features)
    left, right = sides(mid)

    step_total = mod_table.shape[0]
    mods = sum(
        jnp.where((step_index == k)[:, None, None], mod_table[k][None], 0.0)
        for k in range(step_total)
    )
    head_dim = q_gain.shape[0]
    lhs, gram = fold_inputs(embed_weight, mods[:, 1, :], mods[:, 0, :])
    gain = (q_gain * k_gain * (math.log2(math.e) / math.sqrt(head_dim)))[None]
    pair = spread(queries, "row", bits_of("row")[:1])
    pair, lhs = tie((pair, lhs))
    keys = finish_row(pair, queries.shape)
    folded = jnp.dot(lhs, qkv_weight, preferred_element_type=f32)

    def attended(slot, keys, queries, at):
        return attend(keys, queries, slot, at, gram, folded, gain, out_weight)

    parts, sums = {}, {}

    def first(slot):
        keep, send = parts[slot]
        total = keep + exchange(send, "col", 1).astype(f32)
        parts[slot] = (total[0::2], total[1::2].astype(bf16))

    def rest(slot):
        keep, send = parts[slot]
        bit = 2
        while True:
            total = keep + exchange(send, "col", bit).astype(f32)
            if total.shape[0] == 1:
                break
            keep, send = total[0::2], total[1::2].astype(bf16)
            bit *= 2
        sums[slot] = total[0]

    parts[1] = attended(1, keys, queries, 0)
    mid, left, right, parts[1] = tie((mid, left, right, parts[1]))
    latent = encode(left, mid, right, tile_rows, conv_first, conv_second, conv_last)
    channels = latent.shape[-1]
    tok = tile_rows // 2 * (tile_cols // 2)
    patch = (
        latent.reshape(tile_cols // 2, 2, tile_rows // 2, 2, channels)
        .transpose(2, 0, 3, 1, 4)
        .reshape(tok, 4 * channels)
    )
    sigma = (step_total - step_index.astype(f32)) / (step_total + 1.0)
    fresh = ((1.0 - sigma[0]) * patch + sigma[0] * noise.astype(f32)).astype(bf16)
    first(1)
    fresh, queries, parts[1] = tie((fresh, queries, parts[1]))
    fresh_queries = spread(fresh[None], "col", bits_of("col"))
    parts[2] = attended(2, keys, queries, 1)
    fresh_pair = spread(fresh_queries, "row", bits_of("row")[:1])
    fresh_pair, queries, parts[2] = tie((fresh_pair, queries, parts[2]))
    fresh_keys = finish_row(fresh_pair, fresh_queries.shape)
    parts[3] = attended(3, keys, queries, 2)
    rest(1)
    first(2)
    sums[1], parts[2], parts[3] = tie((sums[1], parts[2], parts[3]))
    fresh_queries, parts[2], parts[3] = tie((fresh_queries, parts[2], parts[3]))
    parts[0] = attended(0, fresh_keys, fresh_queries, 0)
    rest(2)
    first(3)
    sums[2], parts[3], parts[0] = tie((sums[2], parts[3], parts[0]))
    first(0)
    rest(3)
    rest(0)

    patches = jnp.concatenate([fresh[None], prior], axis=0)
    own = jnp.einsum(
        "stc,cd->std", patches, embed_weight, preferred_element_type=f32
    ).astype(bf16)
    outs = [
        (own[s].astype(f32) + mods[s, 2][None, :] * sums[s]).astype(bf16) for s in range(slots)
    ]
    return jnp.stack(outs, axis=1)


def solution(mesh):
    placed = (
        P("row", "col", None),
        P(),
        P(),
        P(),
        P(("row", "col"), None),
        P(("row", "col"), None, None),
        P(),
        P(),
        P(),
        P(None, "col"),
        P(),
        P(),
        P("col", None),
    )
    return jax.shard_map(
        on_device,
        mesh=mesh,
        in_specs=placed,
        out_specs=P(("row", "col"), None, None),
        check_vma=False,
    )
```

```python
import functools
import math

import jax
import jax.numpy as jnp
from jax import lax
from jax.experimental import pallas as pl
from jax.experimental.pallas import tpu as pltpu
from jax.sharding import PartitionSpec as P

norm_eps = 1e-06
latent_shift = 0.1159
latent_scale = 0.3611
bf16 = jnp.bfloat16
f32 = jnp.float32


def swish(field):
    return (field / (1.0 + jnp.exp(-field))).astype(bf16)


def shifted(dst_ref, act):
    cols, rows, _ = act.shape
    dst_ref[0, 0:cols] = pltpu.roll(act, 1, 1).astype(bf16)
    dst_ref[1, 0:cols] = act.astype(bf16)
    dst_ref[2, 0:cols] = pltpu.roll(act, rows - 1, 1).astype(bf16)


def encode_kernel(
    place_ref, left_ref, mid_ref, right_ref, f0_ref, f1_ref, f2_ref, s0_ref, s1_ref, s2_ref,
    last_ref, out_ref, x_ref, s_ref, acc_ref,
):
    step = pl.program_id(0)
    wide, rows, channels = x_ref.shape
    tile_cols, tile_rows, _ = out_ref.shape
    first_ref = (f0_ref, f1_ref, f2_ref)
    second_ref = (s0_ref, s1_ref, s2_ref)

    def masked(act, reach):
        shape = act.shape
        col = lax.broadcasted_iota(jnp.int32, shape, 0) + (place_ref[1] - reach)
        row = lax.broadcasted_iota(jnp.int32, shape, 1)
        row = jnp.where(row < tile_rows + 3, row, row - rows) + place_ref[0]
        ok = (row >= 0) & (row < place_ref[2]) & (col >= 0) & (col < place_ref[3])
        return jnp.where(ok, act, 0.0)

    def taps(w_ref, dy, cols):
        total = None
        for dx in range(3):
            lhs = s_ref[dy, dx : dx + cols].reshape(cols * rows, channels)
            part = jnp.dot(lhs, w_ref[dx][...], preferred_element_type=f32)
            total = part if total is None else total + part
        return total.reshape(cols, rows, total.shape[-1])

    @pl.when(step == 0)
    def _():
        x_ref[0:3] = left_ref[...].astype(f32)
        x_ref[3 : 3 + tile_cols] = mid_ref[...].astype(f32)
        x_ref[3 + tile_cols :] = right_ref[...].astype(f32)
        shifted(s_ref, swish(x_ref[...]).astype(f32))
        acc_ref[...] = taps(first_ref, 0, wide - 2)

    for dy in (1, 2):

        @pl.when(step == dy)
        def _():
            acc_ref[...] += taps(first_ref, dy, wide - 2)

    @pl.when(step == 2)
    def _():
        inner = acc_ref[...].astype(bf16).astype(f32)
        shifted(s_ref, masked(swish(inner).astype(f32), 2))

    @pl.when(step == 3)
    def _():
        acc_ref[0 : wide - 4] = x_ref[2 : wide - 2] + taps(second_ref, 0, wide - 4)

    for dy in (1, 2):

        @pl.when(step == 3 + dy)
        def _():
            acc_ref[0 : wide - 4] += taps(second_ref, dy, wide - 4)

    @pl.when(step == 5)
    def _():
        block = acc_ref[0 : wide - 4].astype(bf16).astype(f32)
        shifted(s_ref, masked(swish(block).astype(f32), 1))
        latent = None
        for dy in range(3):
            for dx in range(3):
                lhs = s_ref[dy, dx : dx + wide - 6].reshape(-1, channels)
                part = lax.dot_general(
                    lhs, last_ref[dy, dx], (((1,), (1,)), ((), ())), preferred_element_type=f32
                )
                latent = part if latent is None else latent + part
        latent = ((latent - latent_shift) * latent_scale).reshape(tile_cols, rows, -1)
        out_ref[...] = latent[:, :tile_rows]


def edges(features):
    nr = lax.axis_size("row")
    turned = features.transpose(1, 0, 2)
    tile_cols, tile_rows, channels = turned.shape
    above = lax.ppermute(turned[:, -3:], "row", [(i, i + 1) for i in range(nr - 1)])
    below = lax.ppermute(turned[:, :3], "row", [(i + 1, i) for i in range(nr - 1)])
    spare = -(tile_rows + 6) % 16
    gap = jnp.zeros((tile_cols, spare, channels), bf16)
    return jnp.concatenate([turned, below, gap, above], axis=1)


def sides(mid):
    nc = lax.axis_size("col")
    left = lax.ppermute(mid[-3:], "col", [(i, i + 1) for i in range(nc - 1)])
    right = lax.ppermute(mid[:3], "col", [(i + 1, i) for i in range(nc - 1)])
    return left, right


def encode(left, mid, right, tile_rows, conv_first, conv_second, conv_last):
    nr, nc = lax.axis_size("row"), lax.axis_size("col")
    tile_cols, rows, channels = mid.shape
    wide = tile_cols + 6
    place = jnp.stack(
        [
            lax.axis_index("row") * tile_rows,
            lax.axis_index("col") * tile_cols,
            nr * tile_rows,
            nc * tile_cols,
        ]
    ).astype(jnp.int32)
    hidden = conv_first.shape[3]
    latents = conv_last.shape[3]
    last = conv_last.transpose(0, 1, 3, 2)

    def whole(array):
        return pl.BlockSpec(array.shape, lambda i: (0,) * array.ndim)

    return pl.pallas_call(
        encode_kernel,
        grid=(6,),
        in_specs=[
            pl.BlockSpec(memory_space=pltpu.SMEM),
            whole(left),
            whole(mid),
            whole(right),
            *[
                pl.BlockSpec(
                    (None, None, channels, hidden), lambda i, x=x: (jnp.minimum(i, 2), x, 0, 0)
                )
                for x in range(3)
            ],
            *[
                pl.BlockSpec(
                    (None, None, hidden, channels), lambda i, x=x: (jnp.clip(i - 3, 0, 2), x, 0, 0)
                )
                for x in range(3)
            ],
            whole(last),
        ],
        out_specs=pl.BlockSpec((tile_cols, tile_rows, latents), lambda i: (0, 0, 0)),
        out_shape=jax.ShapeDtypeStruct((tile_cols, tile_rows, latents), f32),
        scratch_shapes=[
            pltpu.VMEM((wide, rows, channels), f32),
            pltpu.VMEM((3, wide, rows, channels), bf16),
            pltpu.VMEM((wide - 2, rows, channels), f32),
        ],
        compiler_params=pltpu.CompilerParams(vmem_limit_bytes=20 * 2**20),
        cost_estimate=pl.CostEstimate(
            flops=2 * 9 * wide * rows * channels * (2 * hidden + latents),
            bytes_accessed=9 * channels * 2 * (2 * hidden + 128),
            transcendentals=3 * wide * rows * channels,
        ),
    )(place, left, mid, right, *[conv_first] * 3, *[conv_second] * 3, last)


def widen(p, gram_ref):
    pf = p.astype(f32)
    pg = jnp.dot(p, gram_ref[0], preferred_element_type=f32)
    pg = pg + jnp.dot(p, gram_ref[1], preferred_element_type=f32)
    var = jnp.sum(pg * pf, axis=1, keepdims=True)
    pn = pf * lax.rsqrt(jnp.maximum(var, 0.0) + norm_eps)
    hi = pn.astype(bf16)
    lo = (pn - hi.astype(f32)).astype(bf16)
    lane = lax.broadcasted_iota(jnp.int32, p.shape, 1)
    ones = jnp.where(lane < 2, 1.0, 0.0).astype(bf16)
    return jnp.concatenate([hi, lo, hi, ones], axis=1)


def attend_kernel(
    hp, head_dim, slot, slots, groups, *refs
):
    key_refs = refs[:groups]
    attend_body(hp, head_dim, slot, slots, key_refs, *refs[groups:])


def attend_body(
    hp, head_dim, slot, slots, key_refs, query_ref, gram_ref, m_ref, bias_ref, gain_ref,
    wo_ref, keep_ref, send_ref, kaug_ref, qaug_ref, att_ref, wo_vmem, sems,
):
    step = pl.program_id(0)
    width = query_ref.shape[-1]
    count = sems.shape[0]
    rows = wo_ref.shape[0] // count
    copies = [
        pltpu.make_async_copy(
            wo_ref.at[i * rows : (i + 1) * rows], wo_vmem.at[i * rows : (i + 1) * rows], sems.at[i]
        )
        for i in range(count)
    ]

    @pl.when(step == 0)
    def _():
        for copy in copies:
            copy.start()
        part = kaug_ref.shape[0] // len(key_refs)
        for i, key_ref in enumerate(key_refs):
            kaug_ref[i * part : (i + 1) * part] = widen(
                key_ref[...].reshape(-1, width), gram_ref
            )
        qaug_ref[...] = widen(query_ref[...].reshape(-1, width), gram_ref)

    kaug = kaug_ref[...]
    qaug = qaug_ref[...]
    outs = []
    for j in range(hp):
        cols = slice(j * 3 * head_dim, (j + 1) * 3 * head_dim)
        m = m_ref[:, cols]
        bias = bias_ref[slot : slot + 1, cols] + bias_ref[slots + slot : slots + slot + 1, cols]
        mhi = m.astype(bf16)
        mlo = (m - mhi.astype(f32)).astype(bf16)
        bhi = bias.astype(bf16).astype(f32)
        blo = bias - bhi
        at = lax.broadcasted_iota(jnp.int32, m.shape, 0)
        low = jnp.where(at == 0, bhi, jnp.where(at == 1, blo, 0.0)).astype(bf16)
        maug = jnp.concatenate([mhi, mhi, mlo, low], axis=0)
        xq = jnp.dot(qaug, maug[:, :head_dim], preferred_element_type=f32)
        xkv = jnp.dot(kaug, maug[:, head_dim:], preferred_element_type=f32)
        xk = xkv[:, :head_dim]
        v = xkv[:, head_dim:].astype(bf16)
        k = (
            xk * lax.rsqrt(jnp.mean(xk * xk, axis=1, keepdims=True) + norm_eps)
        ).astype(bf16)
        q = (
            xq * lax.rsqrt(jnp.mean(xq * xq, axis=1, keepdims=True) + norm_eps) * gain_ref[...]
        ).astype(bf16)
        s = lax.dot_general(q, k, (((1,), (1,)), ((), ())), preferred_element_type=f32)
        e = jnp.exp2(s - jnp.max(s, axis=1, keepdims=True))
        total = jnp.sum(e, axis=1, keepdims=True)
        o = jnp.dot(e.astype(bf16), v, preferred_element_type=f32)
        outs.append((o / total).astype(bf16))
    att_ref[step] = outs[0] if hp == 1 else jnp.concatenate(outs, axis=1)

    @pl.when(step == pl.num_programs(0) - 1)
    def _():
        for copy in copies:
            copy.wait()
        att = jnp.concatenate([att_ref[i] for i in range(att_ref.shape[0])], axis=1)
        part = jnp.dot(att, wo_vmem[...], preferred_element_type=f32)
        tok = keep_ref.shape[1]
        for i in range(keep_ref.shape[0]):
            keep_ref[i] = part[2 * i * tok : (2 * i + 1) * tok, :]
            send_ref[i] = part[(2 * i + 1) * tok : (2 * i + 2) * tok, :].astype(bf16)


def attend(keys, queries, slot, at, gram, folded, gain, out_weight):
    each, nc, _, tok, width = keys[0].shape
    nr = each * len(keys)
    slots = folded.shape[0] // width
    head_dim = gain.shape[1]
    heads = folded.shape[1] // (3 * head_dim)
    depth = out_weight.shape[1]
    hp = heads_per_step(heads)
    nk, nq = nr * nc * tok, nc * tok
    half = nc // 2
    spare = folded.shape[0] - slots * width
    out_spec = pl.BlockSpec((half, tok, depth), lambda h: (0, 0, 0))
    return pl.pallas_call(
        functools.partial(attend_kernel, hp, head_dim, slot, slots, len(keys)),
        grid=(heads // hp,),
        in_specs=[
            *[pl.BlockSpec((each, nc, None, tok, width), lambda h: (0, 0, at, 0, 0))] * len(keys),
            pl.BlockSpec((nc, None, tok, width), lambda h: (0, at, 0, 0)),
            pl.BlockSpec((2, width, width), lambda h: (0, 0, 0)),
            pl.BlockSpec((width, hp * 3 * head_dim), lambda h: (slot, h)),
            pl.BlockSpec((spare, hp * 3 * head_dim), lambda h: (slots * width // spare, h)),
            pl.BlockSpec((1, head_dim), lambda h: (0, 0)),
            pl.BlockSpec(memory_space=pltpu.HBM),
        ],
        out_specs=[out_spec, out_spec],
        out_shape=[
            jax.ShapeDtypeStruct((half, tok, depth), f32),
            jax.ShapeDtypeStruct((half, tok, depth), bf16),
        ],
        scratch_shapes=[
            pltpu.VMEM((nk, 4 * width), bf16),
            pltpu.VMEM((nq, 4 * width), bf16),
            pltpu.VMEM((heads // hp, nq, hp * head_dim), bf16),
            pltpu.VMEM(out_weight.shape, bf16),
            pltpu.SemaphoreType.DMA((3,)),
        ],
        compiler_params=pltpu.CompilerParams(vmem_limit_bytes=16 * 2**20 + 24 * nq * nk),
        cost_estimate=pl.CostEstimate(
            flops=2 * heads * (nk * 256 * 256 + 2 * nq * nk * head_dim * 2 + nq * head_dim * depth),
            bytes_accessed=heads * head_dim * depth * 2 + nq * depth * 3,
            transcendentals=heads * nq * nk,
        ),
    )(*keys, queries, gram, folded, folded, gain, out_weight)


def heads_per_step(heads):
    return max(k for k in (1, 2, 3) if heads % k == 0)


def exchange(value, axis, bit):
    count = lax.axis_size(axis)
    return lax.ppermute(value, axis, [(i, i ^ bit) for i in range(count)])


def reached(value, axis, bits):
    masks = [0]
    for bit in bits:
        masks += [mask | bit for mask in masks]
    return [value] + [exchange(value, axis, mask) for mask in masks[1:]]


def spread(value, axis, bits):
    return jnp.stack(reached(value, axis, bits))


def bits_of(axis):
    return [1 << i for i in range(lax.axis_size(axis).bit_length() - 1)]


def finish_row(keys, shape):
    rest = bits_of("row")[1:]
    while len(rest) > 2:
        keys = spread(keys, "row", rest[:1]).reshape(-1, *shape)
        rest = rest[1:]
    return reached(keys, "row", rest)


def fold_inputs(embed_weight, scale, shift):
    centred = embed_weight.astype(f32)
    centred = centred - jnp.mean(centred, axis=1, keepdims=True)
    width, depth = embed_weight.shape
    slots = scale.shape[0]
    scaled = ((1.0 + scale)[:, None, :] * centred[None]).astype(bf16).reshape(slots * width, depth)
    shift_hi = shift.astype(bf16)
    shift_lo = (shift - shift_hi.astype(f32)).astype(bf16)
    spare = -(2 * slots) % 16
    lhs = jnp.concatenate([scaled, shift_hi, shift_lo, jnp.zeros((spare, depth), bf16)], axis=0)
    gram = jnp.einsum("ad,bd->ab", centred, centred, precision=lax.Precision.HIGHEST) / depth
    gram_hi = gram.astype(bf16)
    return lhs, jnp.stack([gram_hi, (gram - gram_hi.astype(f32)).astype(bf16)])


def on_device(
    features,
    conv_first,
    conv_second,
    conv_last,
    noise,
    prior_patches,
    step_index,
    mod_table,
    embed_weight,
    qkv_weight,
    q_gain,
    k_gain,
    out_weight,
):
    tie = lax.optimization_barrier
    tile_rows, tile_cols, _ = features.shape
    slots = step_index.shape[0]
    prior = prior_patches.transpose(1, 0, 2)
    queries = spread(prior, "col", bits_of("col"))
    mid = edges(features)
    left, right = sides(mid)

    step_total = mod_table.shape[0]
    mods = sum(
        jnp.where((step_index == k)[:, None, None], mod_table[k][None], 0.0)
        for k in range(step_total)
    )
    head_dim = q_gain.shape[0]
    pair = spread(queries, "row", bits_of("row")[:1])
    pair, early_weight, early_mods = tie((pair, embed_weight, mods))
    lhs, gram = fold_inputs(early_weight, early_mods[:, 1, :], early_mods[:, 0, :])
    gain = (q_gain * k_gain * (math.log2(math.e) / math.sqrt(head_dim)))[None]
    keys = finish_row(pair, queries.shape)
    folded = jnp.dot(lhs, qkv_weight, preferred_element_type=f32)

    def attended(slot, keys, queries, at):
        return attend(keys, queries, slot, at, gram, folded, gain, out_weight)

    parts, sums = {}, {}

    def first(slot):
        keep, send = parts[slot]
        total = keep + exchange(send, "col", 1).astype(f32)
        parts[slot] = (total[0::2], total[1::2].astype(bf16))

    def rest(slot):
        keep, send = parts[slot]
        bit = 2
        while True:
            total = keep + exchange(send, "col", bit).astype(f32)
            if total.shape[0] == 1:
                break
            keep, send = total[0::2], total[1::2].astype(bf16)
            bit *= 2
        sums[slot] = total[0]

    mid, left, right, folded = tie((mid, left, right, folded))
    latent = encode(left, mid, right, tile_rows, conv_first, conv_second, conv_last)
    channels = latent.shape[-1]
    tok = tile_rows // 2 * (tile_cols // 2)
    patch = (
        latent.reshape(tile_cols // 2, 2, tile_rows // 2, 2, channels)
        .transpose(2, 0, 3, 1, 4)
        .reshape(tok, 4 * channels)
    )
    sigma = (step_total - step_index.astype(f32)) / (step_total + 1.0)
    fresh = ((1.0 - sigma[0]) * patch + sigma[0] * noise.astype(f32)).astype(bf16)
    arrived = reached(fresh[None], "col", bits_of("col"))
    fresh, queries = tie((fresh, queries))
    parts[1] = attended(1, keys, queries, 0)
    arrived, queries, parts[1] = tie((arrived, queries, parts[1]))
    fresh_queries = jnp.stack(arrived)
    fresh_pair = spread(fresh_queries, "row", bits_of("row")[:1])
    parts[2] = attended(2, keys, queries, 1)
    first(1)
    fresh_pair, queries, parts[1], parts[2] = tie((fresh_pair, queries, parts[1], parts[2]))
    fresh_keys = finish_row(fresh_pair, fresh_queries.shape)
    parts[3] = attended(3, keys, queries, 2)
    first(2)
    fresh_queries, parts[2], parts[3] = tie((fresh_queries, parts[2], parts[3]))
    parts[0] = attended(0, fresh_keys, fresh_queries, 0)
    rest(1)
    first(3)
    sums[1], parts[3], parts[0] = tie((sums[1], parts[3], parts[0]))
    rest(2)
    sums[2], parts[3] = tie((sums[2], parts[3]))
    first(0)
    rest(3)
    rest(0)

    patches = jnp.concatenate([fresh[None], prior], axis=0)
    own = jnp.einsum(
        "stc,cd->std", patches, embed_weight, preferred_element_type=f32
    ).astype(bf16)
    outs = [
        (own[s].astype(f32) + mods[s, 2][None, :] * sums[s]).astype(bf16) for s in range(slots)
    ]
    return jnp.stack(outs, axis=1)


def solution(mesh):
    placed = (
        P("row", "col", None),
        P(),
        P(),
        P(),
        P(("row", "col"), None),
        P(("row", "col"), None, None),
        P(),
        P(),
        P(),
        P(None, "col"),
        P(),
        P(),
        P("col", None),
    )
    return jax.shard_map(
        on_device,
        mesh=mesh,
        in_specs=placed,
        out_specs=P(("row", "col"), None, None),
        check_vma=False,
    )
```

```python
import functools
import math

import jax
import jax.numpy as jnp
from jax import lax
from jax.experimental import pallas as pl
from jax.experimental.pallas import tpu as pltpu
from jax.sharding import PartitionSpec as P

norm_eps = 1e-06
latent_shift = 0.1159
latent_scale = 0.3611
bf16 = jnp.bfloat16
f32 = jnp.float32


def swish(field):
    return (field / (1.0 + jnp.exp(-field))).astype(bf16)


def shifted(dst_ref, act):
    cols, rows, _ = act.shape
    dst_ref[0, 0:cols] = pltpu.roll(act, 1, 1).astype(bf16)
    dst_ref[1, 0:cols] = act.astype(bf16)
    dst_ref[2, 0:cols] = pltpu.roll(act, rows - 1, 1).astype(bf16)


def encode_kernel(
    place_ref, left_ref, mid_ref, right_ref, f0_ref, f1_ref, f2_ref, s0_ref, s1_ref, s2_ref,
    last_ref, out_ref, x_ref, s_ref, acc_ref,
):
    step = pl.program_id(0)
    wide, rows, channels = x_ref.shape
    tile_cols, tile_rows, _ = out_ref.shape
    first_ref = (f0_ref, f1_ref, f2_ref)
    second_ref = (s0_ref, s1_ref, s2_ref)

    def masked(act, reach):
        shape = act.shape
        col = lax.broadcasted_iota(jnp.int32, shape, 0) + (place_ref[1] - reach)
        row = lax.broadcasted_iota(jnp.int32, shape, 1)
        row = jnp.where(row < tile_rows + 3, row, row - rows) + place_ref[0]
        ok = (row >= 0) & (row < place_ref[2]) & (col >= 0) & (col < place_ref[3])
        return jnp.where(ok, act, 0.0)

    def taps(w_ref, dy, cols):
        total = None
        for dx in range(3):
            lhs = s_ref[dy, dx : dx + cols].reshape(cols * rows, channels)
            part = jnp.dot(lhs, w_ref[dx][...], preferred_element_type=f32)
            total = part if total is None else total + part
        return total.reshape(cols, rows, total.shape[-1])

    @pl.when(step == 0)
    def _():
        x_ref[0:3] = left_ref[...].astype(f32)
        x_ref[3 : 3 + tile_cols] = mid_ref[...].astype(f32)
        x_ref[3 + tile_cols :] = right_ref[...].astype(f32)
        shifted(s_ref, swish(x_ref[...]).astype(f32))
        acc_ref[...] = taps(first_ref, 0, wide - 2)

    for dy in (1, 2):

        @pl.when(step == dy)
        def _():
            acc_ref[...] += taps(first_ref, dy, wide - 2)

    @pl.when(step == 2)
    def _():
        inner = acc_ref[...].astype(bf16).astype(f32)
        shifted(s_ref, masked(swish(inner).astype(f32), 2))

    @pl.when(step == 3)
    def _():
        acc_ref[0 : wide - 4] = x_ref[2 : wide - 2] + taps(second_ref, 0, wide - 4)

    for dy in (1, 2):

        @pl.when(step == 3 + dy)
        def _():
            acc_ref[0 : wide - 4] += taps(second_ref, dy, wide - 4)

    @pl.when(step == 5)
    def _():
        block = acc_ref[0 : wide - 4].astype(bf16).astype(f32)
        shifted(s_ref, masked(swish(block).astype(f32), 1))
        latent = None
        for dy in range(3):
            for dx in range(3):
                lhs = s_ref[dy, dx : dx + wide - 6].reshape(-1, channels)
                part = lax.dot_general(
                    lhs, last_ref[dy, dx], (((1,), (1,)), ((), ())), preferred_element_type=f32
                )
                latent = part if latent is None else latent + part
        latent = ((latent - latent_shift) * latent_scale).reshape(tile_cols, rows, -1)
        out_ref[...] = latent[:, :tile_rows]


def edges(features):
    nr = lax.axis_size("row")
    turned = features.transpose(1, 0, 2)
    tile_cols, tile_rows, channels = turned.shape
    above = lax.ppermute(turned[:, -3:], "row", [(i, i + 1) for i in range(nr - 1)])
    below = lax.ppermute(turned[:, :3], "row", [(i + 1, i) for i in range(nr - 1)])
    spare = -(tile_rows + 6) % 16
    gap = jnp.zeros((tile_cols, spare, channels), bf16)
    return jnp.concatenate([turned, below, gap, above], axis=1)


def sides(mid):
    nc = lax.axis_size("col")
    left = lax.ppermute(mid[-3:], "col", [(i, i + 1) for i in range(nc - 1)])
    right = lax.ppermute(mid[:3], "col", [(i + 1, i) for i in range(nc - 1)])
    return left, right


def encode(left, mid, right, tile_rows, conv_first, conv_second, conv_last):
    nr, nc = lax.axis_size("row"), lax.axis_size("col")
    tile_cols, rows, channels = mid.shape
    wide = tile_cols + 6
    place = jnp.stack(
        [
            lax.axis_index("row") * tile_rows,
            lax.axis_index("col") * tile_cols,
            nr * tile_rows,
            nc * tile_cols,
        ]
    ).astype(jnp.int32)
    hidden = conv_first.shape[3]
    latents = conv_last.shape[3]
    last = conv_last.transpose(0, 1, 3, 2)

    def whole(array):
        return pl.BlockSpec(array.shape, lambda i: (0,) * array.ndim)

    return pl.pallas_call(
        encode_kernel,
        grid=(6,),
        in_specs=[
            pl.BlockSpec(memory_space=pltpu.SMEM),
            whole(left),
            whole(mid),
            whole(right),
            *[
                pl.BlockSpec(
                    (None, None, channels, hidden), lambda i, x=x: (jnp.minimum(i, 2), x, 0, 0)
                )
                for x in range(3)
            ],
            *[
                pl.BlockSpec(
                    (None, None, hidden, channels), lambda i, x=x: (jnp.clip(i - 3, 0, 2), x, 0, 0)
                )
                for x in range(3)
            ],
            whole(last),
        ],
        out_specs=pl.BlockSpec((tile_cols, tile_rows, latents), lambda i: (0, 0, 0)),
        out_shape=jax.ShapeDtypeStruct((tile_cols, tile_rows, latents), f32),
        scratch_shapes=[
            pltpu.VMEM((wide, rows, channels), f32),
            pltpu.VMEM((3, wide, rows, channels), bf16),
            pltpu.VMEM((wide - 2, rows, channels), f32),
        ],
        compiler_params=pltpu.CompilerParams(vmem_limit_bytes=20 * 2**20),
        cost_estimate=pl.CostEstimate(
            flops=2 * 9 * wide * rows * channels * (2 * hidden + latents),
            bytes_accessed=9 * channels * 2 * (2 * hidden + 128),
            transcendentals=3 * wide * rows * channels,
        ),
    )(place, left, mid, right, *[conv_first] * 3, *[conv_second] * 3, last)


def widen(p, gram_ref):
    pf = p.astype(f32)
    pg = jnp.dot(p, gram_ref[0], preferred_element_type=f32)
    pg = pg + jnp.dot(p, gram_ref[1], preferred_element_type=f32)
    var = jnp.sum(pg * pf, axis=1, keepdims=True)
    pn = pf * lax.rsqrt(jnp.maximum(var, 0.0) + norm_eps)
    hi = pn.astype(bf16)
    lo = (pn - hi.astype(f32)).astype(bf16)
    lane = lax.broadcasted_iota(jnp.int32, p.shape, 1)
    ones = jnp.where(lane < 2, 1.0, 0.0).astype(bf16)
    return jnp.concatenate([hi, lo, hi, ones], axis=1)


def attend_kernel(
    hp, head_dim, slot, slots, groups, *refs
):
    key_refs = refs[:groups]
    attend_body(hp, head_dim, slot, slots, key_refs, *refs[groups:])


def attend_body(
    hp, head_dim, slot, slots, key_refs, query_ref, gram_ref, m_ref, bias_ref, gain_ref,
    wo_ref, keep_ref, send_ref, kaug_ref, qaug_ref, att_ref, wo_vmem, sems,
):
    step = pl.program_id(0)
    width = query_ref.shape[-1]
    count = sems.shape[0]
    rows = wo_ref.shape[0] // count
    copies = [
        pltpu.make_async_copy(
            wo_ref.at[i * rows : (i + 1) * rows], wo_vmem.at[i * rows : (i + 1) * rows], sems.at[i]
        )
        for i in range(count)
    ]

    @pl.when(step == 0)
    def _():
        for copy in copies:
            copy.start()
        part = kaug_ref.shape[0] // len(key_refs)
        for i, key_ref in enumerate(key_refs):
            kaug_ref[i * part : (i + 1) * part] = widen(
                key_ref[...].reshape(-1, width), gram_ref
            )
        qaug_ref[...] = widen(query_ref[...].reshape(-1, width), gram_ref)

    kaug = kaug_ref[...]
    qaug = qaug_ref[...]
    outs = []
    for j in range(hp):
        cols = slice(j * 3 * head_dim, (j + 1) * 3 * head_dim)
        m = m_ref[:, cols]
        bias = bias_ref[slot : slot + 1, cols] + bias_ref[slots + slot : slots + slot + 1, cols]
        mhi = m.astype(bf16)
        mlo = (m - mhi.astype(f32)).astype(bf16)
        bhi = bias.astype(bf16).astype(f32)
        blo = bias - bhi
        at = lax.broadcasted_iota(jnp.int32, m.shape, 0)
        low = jnp.where(at == 0, bhi, jnp.where(at == 1, blo, 0.0)).astype(bf16)
        maug = jnp.concatenate([mhi, mhi, mlo, low], axis=0)
        xq = jnp.dot(qaug, maug[:, :head_dim], preferred_element_type=f32)
        xkv = jnp.dot(kaug, maug[:, head_dim:], preferred_element_type=f32)
        xk = xkv[:, :head_dim]
        v = xkv[:, head_dim:].astype(bf16)
        k = (
            xk * lax.rsqrt(jnp.mean(xk * xk, axis=1, keepdims=True) + norm_eps)
        ).astype(bf16)
        q = (
            xq * lax.rsqrt(jnp.mean(xq * xq, axis=1, keepdims=True) + norm_eps) * gain_ref[...]
        ).astype(bf16)
        s = lax.dot_general(q, k, (((1,), (1,)), ((), ())), preferred_element_type=f32)
        e = jnp.exp2(s - jnp.max(s, axis=1, keepdims=True))
        total = jnp.sum(e, axis=1, keepdims=True)
        o = jnp.dot(e.astype(bf16), v, preferred_element_type=f32)
        outs.append((o / total).astype(bf16))
    att_ref[step] = outs[0] if hp == 1 else jnp.concatenate(outs, axis=1)

    @pl.when(step == pl.num_programs(0) - 1)
    def _():
        for copy in copies:
            copy.wait()
        att = jnp.concatenate([att_ref[i] for i in range(att_ref.shape[0])], axis=1)
        part = jnp.dot(att, wo_vmem[...], preferred_element_type=f32)
        tok = keep_ref.shape[1]
        for i in range(keep_ref.shape[0]):
            keep_ref[i] = part[2 * i * tok : (2 * i + 1) * tok, :]
            send_ref[i] = part[(2 * i + 1) * tok : (2 * i + 2) * tok, :].astype(bf16)


def attend(keys, queries, slot, at, gram, folded, gain, out_weight):
    each, nc, _, tok, width = keys[0].shape
    nr = each * len(keys)
    slots = folded.shape[0] // width
    head_dim = gain.shape[1]
    heads = folded.shape[1] // (3 * head_dim)
    depth = out_weight.shape[1]
    hp = heads_per_step(heads)
    nk, nq = nr * nc * tok, nc * tok
    half = nc // 2
    spare = folded.shape[0] - slots * width
    out_spec = pl.BlockSpec((half, tok, depth), lambda h: (0, 0, 0))
    return pl.pallas_call(
        functools.partial(attend_kernel, hp, head_dim, slot, slots, len(keys)),
        grid=(heads // hp,),
        in_specs=[
            *[pl.BlockSpec((each, nc, None, tok, width), lambda h: (0, 0, at, 0, 0))] * len(keys),
            pl.BlockSpec((nc, None, tok, width), lambda h: (0, at, 0, 0)),
            pl.BlockSpec((2, width, width), lambda h: (0, 0, 0)),
            pl.BlockSpec((width, hp * 3 * head_dim), lambda h: (slot, h)),
            pl.BlockSpec((spare, hp * 3 * head_dim), lambda h: (slots * width // spare, h)),
            pl.BlockSpec((1, head_dim), lambda h: (0, 0)),
            pl.BlockSpec(memory_space=pltpu.HBM),
        ],
        out_specs=[out_spec, out_spec],
        out_shape=[
            jax.ShapeDtypeStruct((half, tok, depth), f32),
            jax.ShapeDtypeStruct((half, tok, depth), bf16),
        ],
        scratch_shapes=[
            pltpu.VMEM((nk, 4 * width), bf16),
            pltpu.VMEM((nq, 4 * width), bf16),
            pltpu.VMEM((heads // hp, nq, hp * head_dim), bf16),
            pltpu.VMEM(out_weight.shape, bf16),
            pltpu.SemaphoreType.DMA((3,)),
        ],
        compiler_params=pltpu.CompilerParams(vmem_limit_bytes=46 * 2**20),
        cost_estimate=pl.CostEstimate(
            flops=2 * heads * (nk * 256 * 256 + 2 * nq * nk * head_dim * 2 + nq * head_dim * depth),
            bytes_accessed=heads * head_dim * depth * 2 + nq * depth * 3,
            transcendentals=heads * nq * nk,
        ),
    )(*keys, queries, gram, folded, folded, gain, out_weight)


def heads_per_step(heads):
    return max(k for k in (1, 2, 3) if heads % k == 0)


def exchange(value, axis, bit):
    count = lax.axis_size(axis)
    return lax.ppermute(value, axis, [(i, i ^ bit) for i in range(count)])


def reached(value, axis, bits):
    masks = [0]
    for bit in bits:
        masks += [mask | bit for mask in masks]
    return [value] + [exchange(value, axis, mask) for mask in masks[1:]]


def spread(value, axis, bits):
    return jnp.stack(reached(value, axis, bits))


def bits_of(axis):
    return [1 << i for i in range(lax.axis_size(axis).bit_length() - 1)]


def finish_row(keys, shape):
    rest = bits_of("row")[1:]
    while len(rest) > 2:
        keys = spread(keys, "row", rest[:1]).reshape(-1, *shape)
        rest = rest[1:]
    return reached(keys, "row", rest)


def fold_inputs(embed_weight, scale, shift):
    centred = embed_weight.astype(f32)
    centred = centred - jnp.mean(centred, axis=1, keepdims=True)
    width, depth = embed_weight.shape
    slots = scale.shape[0]
    scaled = ((1.0 + scale)[:, None, :] * centred[None]).astype(bf16).reshape(slots * width, depth)
    shift_hi = shift.astype(bf16)
    shift_lo = (shift - shift_hi.astype(f32)).astype(bf16)
    spare = -(2 * slots) % 16
    lhs = jnp.concatenate([scaled, shift_hi, shift_lo, jnp.zeros((spare, depth), bf16)], axis=0)
    gram = jnp.einsum("ad,bd->ab", centred, centred, precision=lax.Precision.HIGHEST) / depth
    gram_hi = gram.astype(bf16)
    return lhs, jnp.stack([gram_hi, (gram - gram_hi.astype(f32)).astype(bf16)])


def on_device(
    features,
    conv_first,
    conv_second,
    conv_last,
    noise,
    prior_patches,
    step_index,
    mod_table,
    embed_weight,
    qkv_weight,
    q_gain,
    k_gain,
    out_weight,
):
    tie = lax.optimization_barrier
    tile_rows, tile_cols, _ = features.shape
    slots = step_index.shape[0]
    prior = prior_patches.transpose(1, 0, 2)
    queries = spread(prior, "col", bits_of("col"))
    mid = edges(features)
    left, right = sides(mid)

    step_total = mod_table.shape[0]
    mods = sum(
        jnp.where((step_index == k)[:, None, None], mod_table[k][None], 0.0)
        for k in range(step_total)
    )
    head_dim = q_gain.shape[0]
    pair = spread(queries, "row", bits_of("row")[:1])
    pair, early_weight, early_mods = tie((pair, embed_weight, mods))
    lhs, gram = fold_inputs(early_weight, early_mods[:, 1, :], early_mods[:, 0, :])
    gain = (q_gain * k_gain * (math.log2(math.e) / math.sqrt(head_dim)))[None]
    keys = finish_row(pair, queries.shape)
    folded = jnp.dot(lhs, qkv_weight, preferred_element_type=f32)

    def attended(slot, keys, queries, at):
        return attend(keys, queries, slot, at, gram, folded, gain, out_weight)

    parts, sums = {}, {}

    def first(slot):
        keep, send = parts[slot]
        total = keep + exchange(send, "col", 1).astype(f32)
        parts[slot] = (total[0::2], total[1::2].astype(bf16))

    def rest(slot):
        keep, send = parts[slot]
        bit = 2
        while True:
            total = keep + exchange(send, "col", bit).astype(f32)
            if total.shape[0] == 1:
                break
            keep, send = total[0::2], total[1::2].astype(bf16)
            bit *= 2
        sums[slot] = total[0]

    mid, left, right, folded = tie((mid, left, right, folded))
    latent = encode(left, mid, right, tile_rows, conv_first, conv_second, conv_last)
    channels = latent.shape[-1]
    tok = tile_rows // 2 * (tile_cols // 2)
    patch = (
        latent.reshape(tile_cols // 2, 2, tile_rows // 2, 2, channels)
        .transpose(2, 0, 3, 1, 4)
        .reshape(tok, 4 * channels)
    )
    sigma = (step_total - step_index.astype(f32)) / (step_total + 1.0)
    fresh = ((1.0 - sigma[0]) * patch + sigma[0] * noise.astype(f32)).astype(bf16)
    arrived = reached(fresh[None], "col", bits_of("col"))
    fresh, queries = tie((fresh, queries))
    parts[1] = attended(1, keys, queries, 0)
    arrived, queries, parts[1] = tie((arrived, queries, parts[1]))
    fresh_queries = jnp.stack(arrived)
    fresh_pair = spread(fresh_queries, "row", bits_of("row")[:1])
    parts[2] = attended(2, keys, queries, 1)
    first(1)
    fresh_pair, queries, parts[1], parts[2] = tie((fresh_pair, queries, parts[1], parts[2]))
    fresh_keys = finish_row(fresh_pair, fresh_queries.shape)
    parts[3] = attended(3, keys, queries, 2)
    first(2)
    fresh_queries, parts[2], parts[3] = tie((fresh_queries, parts[2], parts[3]))
    parts[0] = attended(0, fresh_keys, fresh_queries, 0)
    rest(1)
    first(3)
    sums[1], parts[3], parts[0] = tie((sums[1], parts[3], parts[0]))
    rest(2)
    sums[2], parts[3] = tie((sums[2], parts[3]))
    first(0)
    rest(3)
    rest(0)

    patches = jnp.concatenate([fresh[None], prior], axis=0)
    own = jnp.einsum(
        "stc,cd->std", patches, embed_weight, preferred_element_type=f32
    ).astype(bf16)
    outs = [
        (own[s].astype(f32) + mods[s, 2][None, :] * sums[s]).astype(bf16) for s in range(slots)
    ]
    return jnp.stack(outs, axis=1)


def solution(mesh):
    placed = (
        P("row", "col", None),
        P(),
        P(),
        P(),
        P(("row", "col"), None),
        P(("row", "col"), None, None),
        P(),
        P(),
        P(),
        P(None, "col"),
        P(),
        P(),
        P("col", None),
    )
    return jax.shard_map(
        on_device,
        mesh=mesh,
        in_specs=placed,
        out_specs=P(("row", "col"), None, None),
        check_vma=False,
    )
```
